32 devices in a mesh: pipe: 4 (over y, x), seq: 2 (over core), chan: 4 (over z).
Axes of the slice: x: 2, y: 2, z: 4, core: 2. Of those that a mesh axis runs over, the one named last changes fastest.
Arguments:
- signal: bfloat16 [4, 512, 2048], P('pipe', 'seq', 'chan'), may hold values from -6 to 6
- gate_value: bfloat16 [4, 512, 2048], P('pipe', 'seq', 'chan'), may hold values from -6 to 6
- grad_out: bfloat16 [4, 512, 2048], P('pipe', 'seq', 'chan'), may hold values from -1.5 to 1.5
- long_filter: bfloat16 [4, 512, 2048], P('pipe', 'seq', 'chan'), may hold values from -0.25 to 0.25
- weight: bfloat16 [4, 4096, 2048], P('pipe', None, 'chan'), may hold values from -0.125 to 0.125
Outputs:
- gate_grad: bfloat16 [4, 512, 2048], P('pipe', 'seq', 'chan')
- filter_grad: float32 [4, 512, 2048], P('pipe', 'seq', 'chan')
- input_grad: bfloat16 [4, 512, 4096], P('pipe', 'seq', 'chan')
The draws below stay inside these ranges and needn't reach their ends.
All inputs are finite; a program needn't handle non-finite values.
Results may differ from the reference program's by a relative error of at most 0.02.
Values may be sent and summed in bfloat16 or wider, within the bound.
A program may use at most 128 MiB of HBM per device.

```python
import jax
import jax.numpy as jnp
from jax import lax

D = 4096
CH = 2048
SECTIONS = 4
SEQ_LEN = 512


def block_levels(rng, dims, pieces, low, top_value):
    loudness, own = 1.0, jax.random.fold_in(rng, 6)
    for dim, blocks in pieces:
        draws = jnp.exp(jax.random.uniform(jax.random.fold_in(own, dim), (blocks,), jnp.float32, low / len(pieces), top_value / len(pieces)))
        loudness = loudness * jnp.repeat(draws, dims[dim] // blocks).reshape([-1 if axis == dim else 1 for axis in range(len(dims))])
    return loudness


def normal_values(stream_key, dims, deviation, reach, cuts=(), dtype=jnp.bfloat16):
    factor_of = block_levels(stream_key, dims, cuts, -0.22, 0.18) if cuts else 1.0
    drawn = jax.random.normal(stream_key, dims, jnp.float32) * deviation * factor_of
    return jnp.minimum(jnp.maximum(drawn, -reach), reach).astype(dtype)


def setup_inputs(seed: int = 0) -> dict:
    key_list = jax.random.split(jax.random.key(seed), 6)
    signal = normal_values(key_list[0], (SECTIONS, SEQ_LEN, CH), 1.0, 6.0, ((0, 4), (1, 2), (2, 4)))
    gate_value = normal_values(key_list[1], (SECTIONS, SEQ_LEN, CH), 1.0, 6.0, ((0, 4), (1, 2), (2, 4)))
    grad_out = normal_values(key_list[2], (SECTIONS, SEQ_LEN, CH), 0.25, 1.5, ((0, 4), (1, 2), (2, 4)))
    long_filter = normal_values(key_list[3], (SECTIONS, SEQ_LEN, CH), SEQ_LEN ** -0.5, 0.25, ((0, 4), (1, 2), (2, 4)))
    weight = normal_values(key_list[4], (SECTIONS, D, CH), CH ** -0.5, 0.125, ((0, 4), (2, 4)))
    return dict(signal=signal, gate_value=gate_value, grad_out=grad_out, long_filter=long_filter, weight=weight)


def causal(left_side, right_side):
    seq_length = left_side.shape[0]
    product = jnp.fft.rfft(left_side, 2 * seq_length, axis=0) * jnp.fft.rfft(right_side, 2 * seq_length, axis=0)
    return jnp.fft.irfft(product, 2 * seq_length, axis=0)[:seq_length]


def filter_section(section_items):
    signal, gate_value, grad_out, long_filter = section_items
    signal = signal.astype(jnp.float32)
    grad_wide = grad_out.astype(jnp.float32)
    filter_wide = long_filter.astype(jnp.float32)
    gated_low = (gate_value.astype(jnp.float32) * grad_wide).astype(jnp.bfloat16)
    gated = lax.optimization_barrier(gated_low).astype(jnp.float32)
    conv = causal(filter_wide, signal)
    gate_grad = (grad_wide * conv).astype(jnp.bfloat16)
    signal_grad = causal(filter_wide, gated[::-1])[::-1].astype(jnp.bfloat16)
    filter_grad = causal(signal, gated[::-1])[::-1].astype(jnp.float32)
    return gate_grad, filter_grad, signal_grad


def project_section(section_items):
    received, weight = section_items
    return jnp.dot(received, weight.T, preferred_element_type=jnp.float32).astype(jnp.bfloat16)


def reference(signal, gate_value, grad_out, long_filter, weight):
    gate_grad, filter_grad, signal_grad = lax.map(filter_section, (signal, gate_value, grad_out, long_filter))
    received = jnp.roll(signal_grad, -1, axis=0)
    input_grad = lax.map(project_section, (received, weight))
    return gate_grad, filter_grad, input_grad
```

```python
import functools
import math

import jax
import jax.numpy as jnp
import numpy as np
from jax import lax
from jax.experimental import pallas as pl
from jax.experimental.pallas import tpu as pltpu
from jax.sharding import PartitionSpec as P

HIGHEST = lax.Precision.HIGHEST
HIGHER = lax.Precision.HIGH


def passed_along(x, axis, by):
    length = lax.axis_size(axis)
    return lax.ppermute(x, axis, [(i, (i + by) % length) for i in range(length)])


def make_tables(panel_len):
    span_len = 2 * panel_len
    row_index = lax.broadcasted_iota(jnp.int32, (span_len, panel_len), 0)
    col_index = lax.broadcasted_iota(jnp.int32, (span_len, panel_len), 1)
    frequency = jnp.where(row_index <= panel_len, row_index, row_index - panel_len)
    angles = (frequency * col_index % span_len).astype(jnp.float32) * (2.0 * math.pi / span_len)
    forward_table = jnp.where(row_index <= panel_len, jnp.cos(angles), -jnp.sin(angles))
    end_rows = jnp.logical_or(row_index == 0, row_index == panel_len)
    weights = jnp.where(end_rows, 1.0, 2.0) / span_len
    inverse_table = (forward_table * weights).T
    return (forward_table, inverse_table)


def make_parity(panel_len):
    row_index = lax.broadcasted_iota(jnp.int32, (2 * panel_len, 1), 0)
    frequency = jnp.where(row_index <= panel_len, row_index, row_index - panel_len)
    return (1 - 2 * (frequency % 2)).astype(jnp.float32)


def spec_product(left_spec, right_spec, interior, conjugate):
    panel_len = left_spec.shape[0] // 2
    left_real, left_imag = (left_spec[:panel_len], left_spec[panel_len:])
    right_real, right_imag = (right_spec[:panel_len], right_spec[panel_len:])
    if conjugate:
        right_imag = right_imag * (1.0 - 2.0 * interior)
    real_part = left_real * right_real - interior * left_imag * right_imag
    imag_part = (
        interior * (left_real * right_imag + left_imag * right_real)
        + (1.0 - interior) * left_imag * right_imag
    )
    return jnp.concatenate([real_part, imag_part], axis=0)


def on_device(signal, gate_value, grad_out, long_filter, weight):
    panel_len = signal.shape[1]
    chan_width = signal.shape[2]
    span_len = 2 * panel_len
    panel_count = lax.axis_size("seq")
    my_panel = lax.axis_index("seq")
    forward_table, inverse_table = make_tables(panel_len)
    parity = make_parity(panel_len)
    interior = (lax.broadcasted_iota(jnp.int32, (panel_len, 1), 0) != 0).astype(jnp.float32)
    gated = (gate_value[0].astype(jnp.float32) * grad_out[0].astype(jnp.float32)).astype(
        jnp.bfloat16
    )
    signals, gateds, filters = (
        lax.all_gather(signal, "seq", axis=1, tiled=True),
        lax.all_gather(gated[None], "seq", axis=1, tiled=True),
        lax.all_gather(long_filter, "seq", axis=1, tiled=True),
    )
    zero_spec = jnp.zeros((span_len, chan_width), jnp.float32)

    def spectrum(gathered, panel_at):
        panel_rows = lax.dynamic_slice_in_dim(gathered[0], panel_at * panel_len, panel_len, 0)
        return jnp.dot(forward_table, panel_rows.astype(jnp.float32), precision=HIGHER)

    def spectrum_if(use_panel, gathered, panel_at):
        return lax.cond(
            use_panel,
            lambda where_at: spectrum(gathered, where_at),
            lambda where_at: zero_spec,
            panel_at,
        )

    def invert(spectrum_in):
        return jnp.dot(inverse_table, spectrum_in, precision=HIGHEST)

    def settle(lag_parts, spectrum_in, use_panel, target):

        def add_rows(parts_now):
            row_at = jnp.maximum(target, 0)
            current = lax.dynamic_index_in_dim(parts_now, row_at, 0, keepdims=True)
            return lax.dynamic_update_index_in_dim(
                parts_now, current + invert(spectrum_in)[None], row_at, 0
            )

        return lax.cond(use_panel, add_rows, lambda parts_now: parts_now, lag_parts)

    own_gated = jnp.dot(forward_table, gated.astype(jnp.float32), precision=HIGHER)
    last_lag = jnp.maximum(my_panel, panel_count - 1 - my_panel)
    extras = (
        zero_spec,
        jnp.array(False),
        jnp.zeros((panel_count, panel_len, chan_width), jnp.float32),
    )

    def lag_step(lag_index, loop_state):
        prior_filter, forward_sum, backward_sum, extras_now = loop_state
        filter_now = spectrum(filters, lag_index)
        filter_full = filter_now + parity * prior_filter
        use_forward = lag_index <= my_panel
        use_backward = lag_index <= panel_count - 1 - my_panel
        signal_spec = spectrum_if(use_forward, signals, jnp.maximum(my_panel - lag_index, 0))
        gated_spec = spectrum_if(
            use_backward, gateds, jnp.minimum(my_panel + lag_index, panel_count - 1)
        )
        forward_sum = forward_sum + spec_product(filter_full, signal_spec, interior, False)
        backward_sum = backward_sum + spec_product(gated_spec, filter_full, interior, True)
        prior_pair, prior_flag, lag_parts = extras_now
        pair_spec = spec_product(own_gated, signal_spec, interior, True)
        ready = jnp.logical_and(lag_index >= 1, jnp.logical_or(prior_flag, use_forward))
        lag_parts = settle(lag_parts, prior_pair + parity * pair_spec, ready, lag_index - 1)
        extras_now = (pair_spec, use_forward, lag_parts)
        return (filter_now, forward_sum, backward_sum, extras_now)

    unused_filter, forward_sum, backward_sum, extras = lax.fori_loop(
        0, last_lag + 1, lag_step, (zero_spec, zero_spec, zero_spec, extras)
    )
    prior_pair, prior_flag, lag_parts = extras
    lag_parts = settle(lag_parts, prior_pair, prior_flag, last_lag)
    filter_grad = lax.psum_scatter(
        lag_parts.reshape(1, panel_count * panel_len, chan_width).astype(jnp.bfloat16),
        "seq",
        scatter_dimension=1,
        tiled=True,
    ).astype(jnp.float32)
    conv = invert(forward_sum)
    gate_grad = (grad_out[0].astype(jnp.float32) * conv).astype(jnp.bfloat16)[None]
    signal_grad = invert(backward_sum).astype(jnp.bfloat16)
    received = passed_along(signal_grad[None], "pipe", -1)
    partial_sums = lax.dot_general(
        received[0], weight[0], (((1,), (1,)), ((), ())), preferred_element_type=jnp.float32
    )
    input_grad = lax.psum_scatter(
        partial_sums[None], "chan", scatter_dimension=2, tiled=True
    ).astype(jnp.bfloat16)
    return (gate_grad, filter_grad, input_grad)


MESH = pl.DeviceIdType.MESH
F32 = jnp.float32
BF16 = jnp.bfloat16
CHUNKS = 4


def odd_tables(length):
    steps = np.outer(2 * np.arange(length) + 1, np.arange(length)) % (4 * length)
    angles = steps * (math.pi / (2 * length))
    forward = np.concatenate([np.cos(angles), np.sin(angles)], axis=0)
    return forward.astype(BF16), (forward.T / length).astype(BF16)


def dot(a, b):
    return jnp.dot(a, b, preferred_element_type=F32)


def dot_t(a, b):
    return lax.dot_general(a, b, (((1,), (1,)), ((), ())), preferred_element_type=F32)


def relay_order(groups):
    order = []
    for i in range((groups + 1) // 2):
        order += [groups - 1 - i, i]
    return list(dict.fromkeys(order))


def fused_kernel(
    groups, pipes,
    signal, gate_value, grad_out, long_filter, weight, table, inverse,
    gate_grad, filter_grad, input_grad,
    table_v, inverse_v, weight_v, filter_v, signal_v, gated_v, gate_v, grad_v,
    filter_spec, gated_spec, signal_spec, product, sent_v, received_v,
    parts, from_left, from_right, going, gate_grad_v, filter_grad_v, input_grad_v,
    local_sem, seq_send, seq_recv, pipe_send, pipe_recv, going_sem, left_sem, right_sem, out_sem,
):
    rows, width = gate_v.shape
    freqs = table_v.shape[0] // 2
    chunk = rows // CHUNKS
    outs = going.shape[3]
    me_pipe, me_seq, me = lax.axis_index("pipe"), lax.axis_index("seq"), lax.axis_index("chan")
    before = lax.rem(me_pipe + pipes - 1, pipes)
    after = lax.rem(me_pipe + 1, pipes)
    partner = 1 - me_seq
    last = groups - 1

    barrier = pltpu.get_barrier_semaphore()
    greeted = [{"seq": partner}, {"pipe": before}, {"pipe": after}]
    greeted += [{"chan": lax.rem(me + 1, groups)}, {"chan": lax.rem(me + groups - 1, groups)}]
    for device in greeted:
        pl.semaphore_signal(barrier, inc=1, device_id=device, device_id_type=MESH)

    own = pl.ds(pl.multiple_of(me_seq * rows, rows), rows)

    loads = {}
    for i, (name, src, dst) in enumerate([
        ("gate", gate_value.at[0], gate_v),
        ("grad", grad_out.at[0], grad_v),
        ("filter", long_filter.at[0], filter_v.at[own]),
        ("table", table, table_v),
        ("inverse", inverse.at[own], inverse_v),
        ("signal", signal.at[0], signal_v.at[own]),
        ("weight", weight.at[0], weight_v),
    ]):
        loads[name] = pltpu.make_async_copy(src, dst, local_sem.at[i])
        loads[name].start()

    def to_partner(at, src, dst):
        return pltpu.make_async_remote_copy(
            src_ref=src, dst_ref=dst, send_sem=seq_send.at[at], recv_sem=seq_recv.at[at],
            device_id={"seq": partner}, device_id_type=MESH,
        )

    filter_copy = to_partner(0, long_filter.at[0], filter_v.at[own])
    gated_copy = to_partner(1, gated_v.at[own], gated_v.at[own])
    signal_copy = to_partner(2, signal.at[0], signal_v.at[own])
    pl.semaphore_wait(barrier, len(greeted))
    filter_copy.start()
    loads["gate"].wait()
    loads["grad"].wait()
    gated_v[own, :] = (gate_v[...].astype(F32) * grad_v[...].astype(F32)).astype(BF16)
    gated_copy.start()
    signal_copy.start()

    tile = min(256, width)
    tiles = [
        (pl.ds(f, tile), pl.ds(freqs + f, tile), pl.ds(c, tile))
        for c in range(0, width, tile)
        for f in range(0, freqs, tile)
    ]
    loads["table"].wait()
    loads["filter"].wait()
    filter_copy.wait_recv()
    for re, im, ch in tiles:
        filter_spec[re, ch] = dot(table_v[re, :], filter_v[:, ch])
        filter_spec[im, ch] = dot(table_v[im, :], filter_v[:, ch])
    gated_copy.wait_recv()
    for re, im, ch in tiles:
        g_re, g_im = dot(table_v[re, :], gated_v[:, ch]), dot(table_v[im, :], gated_v[:, ch])
        h_re, h_im = filter_spec[re, ch], filter_spec[im, ch]
        gated_spec[re, ch] = g_re
        gated_spec[im, ch] = g_im
        product[re, ch] = (h_re * g_re + h_im * g_im).astype(BF16)
        product[im, ch] = (h_re * g_im - h_im * g_re).astype(BF16)
    loads["inverse"].wait()

    def piece(r):
        return pl.ds(r * chunk, chunk)

    passed = [
        pltpu.make_async_remote_copy(
            src_ref=sent_v.at[piece(r)], dst_ref=received_v.at[piece(r)],
            send_sem=pipe_send.at[r], recv_sem=pipe_recv.at[r],
            device_id={"pipe": before}, device_id_type=MESH,
        )
        for r in range(CHUNKS)
    ]
    half = rows // 2
    for h in range(2):
        at = pl.ds(h * half, half)
        sent_v[at, :] = dot(inverse_v[at, :], product[...]).astype(BF16)
        for r in range(h * CHUNKS // 2, (h + 1) * CHUNKS // 2):
            passed[r].start()

    loads["signal"].wait()
    signal_copy.wait_recv()

    def convolve():
        for re, im, ch in tiles:
            s_re, s_im = dot(table_v[re, :], signal_v[:, ch]), dot(table_v[im, :], signal_v[:, ch])
            h_re, h_im = filter_spec[re, ch], filter_spec[im, ch]
            signal_spec[re, ch] = s_re
            signal_spec[im, ch] = s_im
            product[re, ch] = (h_re * s_re - h_im * s_im).astype(BF16)
            product[im, ch] = (h_re * s_im + h_im * s_re).astype(BF16)
        conv = dot(inverse_v[...], product[...])
        gate_grad_v[...] = (grad_v[...].astype(F32) * conv).astype(BF16)
        gate_grad_out.start()

    def correlate():
        for re, im, ch in tiles:
            s_re, s_im = signal_spec[re, ch], signal_spec[im, ch]
            g_re, g_im = gated_spec[re, ch], gated_spec[im, ch]
            product[re, ch] = (s_re * g_re + s_im * g_im).astype(BF16)
            product[im, ch] = (s_re * g_im - s_im * g_re).astype(BF16)
        filter_grad_v[...] = dot(inverse_v[...], product[...])
        filter_grad_out.start()

    gate_grad_out = pltpu.make_async_copy(gate_grad_v, gate_grad.at[0], out_sem.at[0])
    filter_grad_out = pltpu.make_async_copy(filter_grad_v, filter_grad.at[0], out_sem.at[1])
    input_grad_out = [
        pltpu.make_async_copy(
            input_grad_v.at[piece(r)], input_grad.at[0, piece(r)], out_sem.at[2 + r]
        )
        for r in range(CHUNKS)
    ]

    def rightward(r, d):
        return pltpu.make_async_remote_copy(
            src_ref=going.at[r, d], dst_ref=from_left.at[r, d],
            send_sem=going_sem.at[r, d], recv_sem=left_sem.at[r, d],
            device_id={"chan": lax.rem(me + 1, groups)}, device_id_type=MESH,
        )

    def leftward(r, d):
        return pltpu.make_async_remote_copy(
            src_ref=going.at[r, d], dst_ref=from_right.at[r, d],
            send_sem=going_sem.at[r, d], recv_sem=right_sem.at[r, d],
            device_id={"chan": lax.rem(me + groups - 1, groups)}, device_id_type=MESH,
        )

    def multiply(r):
        passed[r].wait_recv()
        block = received_v[piece(r), :]
        for j in range(groups):
            d = jnp.where(2 * me < groups, last - j, j)
            at = pl.ds(pl.multiple_of(d * outs, outs), outs)
            parts[r, d] = dot_t(block, weight_v[at, :])

            @pl.when(jnp.logical_and(me == 0, d > 0))
            def _():
                going[r, d] = parts[r, d].astype(BF16)
                rightward(r, d).start()

            @pl.when(jnp.logical_and(me == last, d < last))
            def _():
                going[r, d] = parts[r, d].astype(BF16)
                leftward(r, d).start()

    def relay(r):
        for d in relay_order(groups):
            @pl.when(jnp.logical_and(me > 0, me < d))
            def _():
                rightward(r, d).wait_recv()
                going[r, d] = (parts[r, d] + from_left[r, d].astype(F32)).astype(BF16)
                rightward(r, d).start()

            @pl.when(jnp.logical_and(me < last, me > d))
            def _():
                leftward(r, d).wait_recv()
                going[r, d] = (parts[r, d] + from_right[r, d].astype(F32)).astype(BF16)
                leftward(r, d).start()

    def finish(r):
        @pl.when(me > 0)
        def _():
            rightward(r, me).wait_recv()
            parts[r, me] = parts[r, me] + from_left[r, me].astype(F32)

        @pl.when(me < last)
        def _():
            leftward(r, me).wait_recv()
            parts[r, me] = parts[r, me] + from_right[r, me].astype(F32)

        input_grad_v[piece(r), :] = parts[r, me].astype(BF16)
        input_grad_out[r].start()

    convolve()
    loads["weight"].wait()
    for r in range(CHUNKS):
        multiply(r)
        if r == 1:
            correlate()
        if r > 0:
            relay(r - 1)
    finish(0)
    relay(CHUNKS - 1)
    for r in range(1, CHUNKS):
        finish(r)

    for copy in (filter_copy, gated_copy, signal_copy, *passed):
        copy.wait_send()
    for r in range(CHUNKS):
        for d in range(groups):
            @pl.when(me != d)
            def _():
                rightward(r, d).wait_send()
    gate_grad_out.wait()
    filter_grad_out.wait()
    for copy in input_grad_out:
        copy.wait()


def fused(signal, gate_value, grad_out, long_filter, weight):
    groups, pipes = lax.axis_size("chan"), lax.axis_size("pipe")
    _, rows, width = signal.shape
    length = 2 * rows
    model = weight.shape[1]
    outs, chunk = model // groups, rows // CHUNKS
    forward, inverse = odd_tables(length)
    moved = pltpu.VMEM((CHUNKS, groups, chunk, outs), BF16)
    spec = pltpu.VMEM((2 * length, width), F32)
    panel = pltpu.VMEM((rows, width), BF16)
    whole = pltpu.VMEM((length, width), BF16)
    sems = pltpu.SemaphoreType.DMA
    anywhere = pl.BlockSpec(memory_space=pl.ANY)
    macs = 6 * 2 * length * length * width + rows * width * model
    return pl.pallas_call(
        functools.partial(fused_kernel, groups, pipes),
        out_shape=(
            jax.ShapeDtypeStruct((1, rows, width), BF16),
            jax.ShapeDtypeStruct((1, rows, width), F32),
            jax.ShapeDtypeStruct((1, rows, outs), BF16),
        ),
        in_specs=[anywhere] * 7,
        out_specs=(anywhere,) * 3,
        scratch_shapes=[
            pltpu.VMEM((2 * length, length), BF16),
            pltpu.VMEM((rows, 2 * length), BF16),
            pltpu.VMEM((model, width), BF16),
            whole, whole, whole, panel, panel,
            spec, spec, spec,
            pltpu.VMEM((2 * length, width), BF16),
            panel, panel,
            pltpu.VMEM((CHUNKS, groups, chunk, outs), F32),
            moved, moved, moved,
            panel,
            pltpu.VMEM((rows, width), F32),
            pltpu.VMEM((rows, outs), BF16),
            sems((7,)), sems((3,)), sems((3,)), sems((CHUNKS,)), sems((CHUNKS,)),
            sems((CHUNKS, groups)), sems((CHUNKS, groups)), sems((CHUNKS, groups)),
            sems((2 + CHUNKS,)),
        ],
        compiler_params=pltpu.CompilerParams(
            collective_id=0, has_side_effects=True, vmem_limit_bytes=48 * 1024 * 1024
        ),
        cost_estimate=pl.CostEstimate(flops=2 * macs, bytes_accessed=2 * model * width, transcendentals=0),
    )(signal, gate_value, grad_out, long_filter, weight, jnp.asarray(forward), jnp.asarray(inverse))


def solution(mesh):
    return jax.shard_map(
        fused if mesh.shape["seq"] == 2 else on_device,
        mesh=mesh,
        in_specs=(
            P("pipe", "seq", "chan"),
            P("pipe", "seq", "chan"),
            P("pipe", "seq", "chan"),
            P("pipe", "seq", "chan"),
            P("pipe", None, "chan"),
        ),
        out_specs=(P("pipe", "seq", "chan"), P("pipe", "seq", "chan"), P("pipe", "seq", "chan")),
        check_vma=False,
    )
```

```python
import functools
import math

import jax
import jax.numpy as jnp
import numpy as np
from jax import lax
from jax.experimental import pallas as pl
from jax.experimental.pallas import tpu as pltpu
from jax.sharding import PartitionSpec as P

HIGHEST = lax.Precision.HIGHEST
HIGHER = lax.Precision.HIGH


def passed_along(x, axis, by):
    length = lax.axis_size(axis)
    return lax.ppermute(x, axis, [(i, (i + by) % length) for i in range(length)])


def make_tables(panel_len):
    span_len = 2 * panel_len
    row_index = lax.broadcasted_iota(jnp.int32, (span_len, panel_len), 0)
    col_index = lax.broadcasted_iota(jnp.int32, (span_len, panel_len), 1)
    frequency = jnp.where(row_index <= panel_len, row_index, row_index - panel_len)
    angles = (frequency * col_index % span_len).astype(jnp.float32) * (2.0 * math.pi / span_len)
    forward_table = jnp.where(row_index <= panel_len, jnp.cos(angles), -jnp.sin(angles))
    end_rows = jnp.logical_or(row_index == 0, row_index == panel_len)
    weights = jnp.where(end_rows, 1.0, 2.0) / span_len
    inverse_table = (forward_table * weights).T
    return (forward_table, inverse_table)


def make_parity(panel_len):
    row_index = lax.broadcasted_iota(jnp.int32, (2 * panel_len, 1), 0)
    frequency = jnp.where(row_index <= panel_len, row_index, row_index - panel_len)
    return (1 - 2 * (frequency % 2)).astype(jnp.float32)


def spec_product(left_spec, right_spec, interior, conjugate):
    panel_len = left_spec.shape[0] // 2
    left_real, left_imag = (left_spec[:panel_len], left_spec[panel_len:])
    right_real, right_imag = (right_spec[:panel_len], right_spec[panel_len:])
    if conjugate:
        right_imag = right_imag * (1.0 - 2.0 * interior)
    real_part = left_real * right_real - interior * left_imag * right_imag
    imag_part = (
        interior * (left_real * right_imag + left_imag * right_real)
        + (1.0 - interior) * left_imag * right_imag
    )
    return jnp.concatenate([real_part, imag_part], axis=0)


def on_device(signal, gate_value, grad_out, long_filter, weight):
    panel_len = signal.shape[1]
    chan_width = signal.shape[2]
    span_len = 2 * panel_len
    panel_count = lax.axis_size("seq")
    my_panel = lax.axis_index("seq")
    forward_table, inverse_table = make_tables(panel_len)
    parity = make_parity(panel_len)
    interior = (lax.broadcasted_iota(jnp.int32, (panel_len, 1), 0) != 0).astype(jnp.float32)
    gated = (gate_value[0].astype(jnp.float32) * grad_out[0].astype(jnp.float32)).astype(
        jnp.bfloat16
    )
    signals, gateds, filters = (
        lax.all_gather(signal, "seq", axis=1, tiled=True),
        lax.all_gather(gated[None], "seq", axis=1, tiled=True),
        lax.all_gather(long_filter, "seq", axis=1, tiled=True),
    )
    zero_spec = jnp.zeros((span_len, chan_width), jnp.float32)

    def spectrum(gathered, panel_at):
        panel_rows = lax.dynamic_slice_in_dim(gathered[0], panel_at * panel_len, panel_len, 0)
        return jnp.dot(forward_table, panel_rows.astype(jnp.float32), precision=HIGHER)

    def spectrum_if(use_panel, gathered, panel_at):
        return lax.cond(
            use_panel,
            lambda where_at: spectrum(gathered, where_at),
            lambda where_at: zero_spec,
            panel_at,
        )

    def invert(spectrum_in):
        return jnp.dot(inverse_table, spectrum_in, precision=HIGHEST)

    def settle(lag_parts, spectrum_in, use_panel, target):

        def add_rows(parts_now):
            row_at = jnp.maximum(target, 0)
            current = lax.dynamic_index_in_dim(parts_now, row_at, 0, keepdims=True)
            return lax.dynamic_update_index_in_dim(
                parts_now, current + invert(spectrum_in)[None], row_at, 0
            )

        return lax.cond(use_panel, add_rows, lambda parts_now: parts_now, lag_parts)

    own_gated = jnp.dot(forward_table, gated.astype(jnp.float32), precision=HIGHER)
    last_lag = jnp.maximum(my_panel, panel_count - 1 - my_panel)
    extras = (
        zero_spec,
        jnp.array(False),
        jnp.zeros((panel_count, panel_len, chan_width), jnp.float32),
    )

    def lag_step(lag_index, loop_state):
        prior_filter, forward_sum, backward_sum, extras_now = loop_state
        filter_now = spectrum(filters, lag_index)
        filter_full = filter_now + parity * prior_filter
        use_forward = lag_index <= my_panel
        use_backward = lag_index <= panel_count - 1 - my_panel
        signal_spec = spectrum_if(use_forward, signals, jnp.maximum(my_panel - lag_index, 0))
        gated_spec = spectrum_if(
            use_backward, gateds, jnp.minimum(my_panel + lag_index, panel_count - 1)
        )
        forward_sum = forward_sum + spec_product(filter_full, signal_spec, interior, False)
        backward_sum = backward_sum + spec_product(gated_spec, filter_full, interior, True)
        prior_pair, prior_flag, lag_parts = extras_now
        pair_spec = spec_product(own_gated, signal_spec, interior, True)
        ready = jnp.logical_and(lag_index >= 1, jnp.logical_or(prior_flag, use_forward))
        lag_parts = settle(lag_parts, prior_pair + parity * pair_spec, ready, lag_index - 1)
        extras_now = (pair_spec, use_forward, lag_parts)
        return (filter_now, forward_sum, backward_sum, extras_now)

    unused_filter, forward_sum, backward_sum, extras = lax.fori_loop(
        0, last_lag + 1, lag_step, (zero_spec, zero_spec, zero_spec, extras)
    )
    prior_pair, prior_flag, lag_parts = extras
    lag_parts = settle(lag_parts, prior_pair, prior_flag, last_lag)
    filter_grad = lax.psum_scatter(
        lag_parts.reshape(1, panel_count * panel_len, chan_width).astype(jnp.bfloat16),
        "seq",
        scatter_dimension=1,
        tiled=True,
    ).astype(jnp.float32)
    conv = invert(forward_sum)
    gate_grad = (grad_out[0].astype(jnp.float32) * conv).astype(jnp.bfloat16)[None]
    signal_grad = invert(backward_sum).astype(jnp.bfloat16)
    received = passed_along(signal_grad[None], "pipe", -1)
    partial_sums = lax.dot_general(
        received[0], weight[0], (((1,), (1,)), ((), ())), preferred_element_type=jnp.float32
    )
    input_grad = lax.psum_scatter(
        partial_sums[None], "chan", scatter_dimension=2, tiled=True
    ).astype(jnp.bfloat16)
    return (gate_grad, filter_grad, input_grad)


MESH = pl.DeviceIdType.MESH
F32 = jnp.float32
BF16 = jnp.bfloat16
CHUNKS = 4
VMEM_BYTES = 62 * 1024 * 1024


def odd_tables(length):
    steps = np.outer(2 * np.arange(length) + 1, np.arange(length)) % (4 * length)
    angles = steps * (math.pi / (2 * length))
    forward = np.concatenate([np.cos(angles), np.sin(angles)], axis=0)
    return forward.astype(BF16), (forward.T / length).astype(BF16)


def dot(a, b):
    return jnp.dot(a, b, preferred_element_type=F32)


def dot_t(a, b):
    return lax.dot_general(a, b, (((1,), (1,)), ((), ())), preferred_element_type=F32)


def relay_order(groups):
    order = []
    for i in range((groups + 1) // 2):
        order += [groups - 1 - i, i]
    return list(dict.fromkeys(order))


def fused_kernel(
    groups, pipes,
    signal, gate_value, grad_out, long_filter, weight, table, inverse,
    gate_grad, filter_grad, input_grad,
    table_v, inverse_v, weight_v, filter_v, signal_v, gated_v, gate_v, grad_v,
    filter_spec, gated_spec, signal_spec, product, sent_v, received_v,
    parts, from_left, from_right, going, gate_grad_v, filter_grad_v, input_grad_v,
    local_sem, seq_send, seq_recv, pipe_send, pipe_recv, going_sem, left_sem, right_sem, out_sem,
):
    rows, width = gate_v.shape
    freqs = table_v.shape[0] // 2
    chunk = rows // CHUNKS
    outs = going.shape[3]
    me_pipe, me_seq, me = lax.axis_index("pipe"), lax.axis_index("seq"), lax.axis_index("chan")
    before = lax.rem(me_pipe + pipes - 1, pipes)
    after = lax.rem(me_pipe + 1, pipes)
    partner = 1 - me_seq
    last = groups - 1

    barrier = pltpu.get_barrier_semaphore()
    greeted = [{"seq": partner}, {"pipe": before}, {"pipe": after}]
    greeted += [{"chan": lax.rem(me + 1, groups)}, {"chan": lax.rem(me + groups - 1, groups)}]
    for device in greeted:
        pl.semaphore_signal(barrier, inc=1, device_id=device, device_id_type=MESH)

    own = pl.ds(pl.multiple_of(me_seq * rows, rows), rows)

    loads = {}
    for i, (name, src, dst) in enumerate([
        ("gate", gate_value.at[0], gate_v),
        ("grad", grad_out.at[0], grad_v),
        ("filter", long_filter.at[0], filter_v.at[own]),
        ("table", table, table_v),
        ("inverse", inverse.at[own], inverse_v),
        ("signal", signal.at[0], signal_v.at[own]),
        ("weight", weight.at[0], weight_v),
    ]):
        loads[name] = pltpu.make_async_copy(src, dst, local_sem.at[i])
        loads[name].start()

    def to_partner(at, src, dst):
        return pltpu.make_async_remote_copy(
            src_ref=src, dst_ref=dst, send_sem=seq_send.at[at], recv_sem=seq_recv.at[at],
            device_id={"seq": partner}, device_id_type=MESH,
        )

    filter_copy = to_partner(0, long_filter.at[0], filter_v.at[own])
    gated_copy = to_partner(1, gated_v.at[own], gated_v.at[own])
    signal_copy = to_partner(2, signal.at[0], signal_v.at[own])
    pl.semaphore_wait(barrier, len(greeted))
    filter_copy.start()
    loads["gate"].wait()
    loads["grad"].wait()
    gated_v[own, :] = (gate_v[...].astype(F32) * grad_v[...].astype(F32)).astype(BF16)
    gated_copy.start()
    signal_copy.start()

    tile = min(256, width)
    tiles = [
        (pl.ds(f, tile), pl.ds(freqs + f, tile), pl.ds(c, tile))
        for c in range(0, width, tile)
        for f in range(0, freqs, tile)
    ]
    loads["table"].wait()
    loads["filter"].wait()
    filter_copy.wait_recv()
    for re, im, ch in tiles:
        filter_spec[re, ch] = dot(table_v[re, :], filter_v[:, ch])
        filter_spec[im, ch] = dot(table_v[im, :], filter_v[:, ch])
    gated_copy.wait_recv()
    for re, im, ch in tiles:
        g_re, g_im = dot(table_v[re, :], gated_v[:, ch]), dot(table_v[im, :], gated_v[:, ch])
        h_re, h_im = filter_spec[re, ch], filter_spec[im, ch]
        gated_spec[re, ch] = g_re
        gated_spec[im, ch] = g_im
        product[re, ch] = (h_re * g_re + h_im * g_im).astype(BF16)
        product[im, ch] = (h_re * g_im - h_im * g_re).astype(BF16)
    loads["inverse"].wait()

    def piece(r):
        return pl.ds(r * chunk, chunk)

    passed = [
        pltpu.make_async_remote_copy(
            src_ref=sent_v.at[piece(r)], dst_ref=received_v.at[piece(r)],
            send_sem=pipe_send.at[r], recv_sem=pipe_recv.at[r],
            device_id={"pipe": before}, device_id_type=MESH,
        )
        for r in range(CHUNKS)
    ]
    half = rows // 2
    for h in range(2):
        at = pl.ds(h * half, half)
        sent_v[at, :] = dot(inverse_v[at, :], product[...]).astype(BF16)
        for r in range(h * CHUNKS // 2, (h + 1) * CHUNKS // 2):
            passed[r].start()

    loads["signal"].wait()
    signal_copy.wait_recv()

    def convolve_start():
        for re, im, ch in tiles:
            s_re, s_im = dot(table_v[re, :], signal_v[:, ch]), dot(table_v[im, :], signal_v[:, ch])
            h_re, h_im = filter_spec[re, ch], filter_spec[im, ch]
            signal_spec[re, ch] = s_re
            signal_spec[im, ch] = s_im
            product[re, ch] = (h_re * s_re - h_im * s_im).astype(BF16)
            product[im, ch] = (h_re * s_im + h_im * s_re).astype(BF16)

    def convolve_end():
        conv = dot(inverse_v[...], product[...])
        gate_grad_v[...] = (grad_v[...].astype(F32) * conv).astype(BF16)
        gate_grad_out.start()

    def correlate():
        for re, im, ch in tiles:
            s_re, s_im = signal_spec[re, ch], signal_spec[im, ch]
            g_re, g_im = gated_spec[re, ch], gated_spec[im, ch]
            product[re, ch] = (s_re * g_re + s_im * g_im).astype(BF16)
            product[im, ch] = (s_re * g_im - s_im * g_re).astype(BF16)
        filter_grad_v[...] = dot(inverse_v[...], product[...])
        filter_grad_out.start()

    gate_grad_out = pltpu.make_async_copy(gate_grad_v, gate_grad.at[0], out_sem.at[0])
    filter_grad_out = pltpu.make_async_copy(filter_grad_v, filter_grad.at[0], out_sem.at[1])
    input_grad_out = [
        pltpu.make_async_copy(
            input_grad_v.at[piece(r)], input_grad.at[0, piece(r)], out_sem.at[2 + r]
        )
        for r in range(CHUNKS)
    ]

    def rightward(r, d):
        return pltpu.make_async_remote_copy(
            src_ref=going.at[r, d], dst_ref=from_left.at[r, d],
            send_sem=going_sem.at[r, d], recv_sem=left_sem.at[r, d],
            device_id={"chan": lax.rem(me + 1, groups)}, device_id_type=MESH,
        )

    def leftward(r, d):
        return pltpu.make_async_remote_copy(
            src_ref=going.at[r, d], dst_ref=from_right.at[r, d],
            send_sem=going_sem.at[r, d], recv_sem=right_sem.at[r, d],
            device_id={"chan": lax.rem(me + groups - 1, groups)}, device_id_type=MESH,
        )

    def multiply(r):
        passed[r].wait_recv()
        block = received_v[piece(r), :]
        for j in range(groups):
            d = jnp.where(2 * me < groups, last - j, j)
            at = pl.ds(pl.multiple_of(d * outs, outs), outs)
            parts[r, d] = dot_t(block, weight_v[at, :])

            @pl.when(jnp.logical_and(me == 0, d > 0))
            def _():
                going[r, d] = parts[r, d].astype(BF16)
                rightward(r, d).start()

            @pl.when(jnp.logical_and(me == last, d < last))
            def _():
                going[r, d] = parts[r, d].astype(BF16)
                leftward(r, d).start()

    def relay(r):
        for d in relay_order(groups):
            @pl.when(jnp.logical_and(me > 0, me < d))
            def _():
                rightward(r, d).wait_recv()
                going[r, d] = (parts[r, d] + from_left[r, d].astype(F32)).astype(BF16)
                rightward(r, d).start()

            @pl.when(jnp.logical_and(me < last, me > d))
            def _():
                leftward(r, d).wait_recv()
                going[r, d] = (parts[r, d] + from_right[r, d].astype(F32)).astype(BF16)
                leftward(r, d).start()

    def finish(r):
        @pl.when(me > 0)
        def _():
            rightward(r, me).wait_recv()
            parts[r, me] = parts[r, me] + from_left[r, me].astype(F32)

        @pl.when(me < last)
        def _():
            leftward(r, me).wait_recv()
            parts[r, me] = parts[r, me] + from_right[r, me].astype(F32)

        input_grad_v[piece(r), :] = parts[r, me].astype(BF16)
        input_grad_out[r].start()

    convolve_start()
    loads["weight"].wait()
    for r in range(CHUNKS):
        multiply(r)
        if r == 1:
            convolve_end()
            correlate()
        if r > 0:
            relay(r - 1)
    finish(0)
    relay(CHUNKS - 1)
    for r in range(1, CHUNKS):
        finish(r)

    for copy in (filter_copy, gated_copy, signal_copy, *passed):
        copy.wait_send()
    for r in range(CHUNKS):
        for d in range(groups):
            @pl.when(me != d)
            def _():
                rightward(r, d).wait_send()
    gate_grad_out.wait()
    filter_grad_out.wait()
    for copy in input_grad_out:
        copy.wait()


def settle_kernel(*refs):
    count = (len(refs) - 1) // 2
    sources, targets, sems = refs[:count], refs[count : 2 * count], refs[-1]
    copies = [pltpu.make_async_copy(sources[i], targets[i], sems.at[i]) for i in range(count)]
    for copy in copies:
        copy.start()
    for copy in copies:
        copy.wait()


def settled(arrays):
    anywhere = pl.BlockSpec(memory_space=pl.ANY)
    return pl.pallas_call(
        settle_kernel,
        out_shape=tuple(jax.ShapeDtypeStruct(x.shape, x.dtype) for x in arrays),
        in_specs=[anywhere] * len(arrays),
        out_specs=(anywhere,) * len(arrays),
        scratch_shapes=[pltpu.SemaphoreType.DMA((len(arrays),))],
        compiler_params=pltpu.CompilerParams(vmem_limit_bytes=VMEM_BYTES),
    )(*arrays)


def fused(signal, gate_value, grad_out, long_filter, weight):
    groups, pipes = lax.axis_size("chan"), lax.axis_size("pipe")
    _, rows, width = signal.shape
    length = 2 * rows
    model = weight.shape[1]
    outs, chunk = model // groups, rows // CHUNKS
    forward, inverse = odd_tables(length)
    moved = pltpu.VMEM((CHUNKS, groups, chunk, outs), BF16)
    spec = pltpu.VMEM((2 * length, width), F32)
    panel = pltpu.VMEM((rows, width), BF16)
    whole = pltpu.VMEM((length, width), BF16)
    sems = pltpu.SemaphoreType.DMA
    anywhere = pl.BlockSpec(memory_space=pl.ANY)
    macs = 6 * 2 * length * length * width + rows * width * model
    grads = pl.pallas_call(
        functools.partial(fused_kernel, groups, pipes),
        out_shape=(
            jax.ShapeDtypeStruct((1, rows, width), BF16),
            jax.ShapeDtypeStruct((1, rows, width), F32),
            jax.ShapeDtypeStruct((1, rows, outs), BF16),
        ),
        in_specs=[anywhere] * 7,
        out_specs=(anywhere,) * 3,
        scratch_shapes=[
            pltpu.VMEM((2 * length, length), BF16),
            pltpu.VMEM((rows, 2 * length), BF16),
            pltpu.VMEM((model, width), BF16),
            whole, whole, whole, panel, panel,
            spec, spec, spec,
            pltpu.VMEM((2 * length, width), BF16),
            panel, panel,
            pltpu.VMEM((CHUNKS, groups, chunk, outs), F32),
            moved, moved, moved,
            panel,
            pltpu.VMEM((rows, width), F32),
            pltpu.VMEM((rows, outs), BF16),
            sems((7,)), sems((3,)), sems((3,)), sems((CHUNKS,)), sems((CHUNKS,)),
            sems((CHUNKS, groups)), sems((CHUNKS, groups)), sems((CHUNKS, groups)),
            sems((2 + CHUNKS,)),
        ],
        compiler_params=pltpu.CompilerParams(
            collective_id=0, has_side_effects=True, vmem_limit_bytes=VMEM_BYTES
        ),
        cost_estimate=pl.CostEstimate(flops=2 * macs, bytes_accessed=2 * model * width, transcendentals=0),
    )(signal, gate_value, grad_out, long_filter, weight, jnp.asarray(forward), jnp.asarray(inverse))
    return settled(grads)


def solution(mesh):
    return jax.shard_map(
        fused if mesh.shape["seq"] == 2 else on_device,
        mesh=mesh,
        in_specs=(
            P("pipe", "seq", "chan"),
            P("pipe", "seq", "chan"),
            P("pipe", "seq", "chan"),
            P("pipe", "seq", "chan"),
            P("pipe", None, "chan"),
        ),
        out_specs=(P("pipe", "seq", "chan"), P("pipe", "seq", "chan"), P("pipe", "seq", "chan")),
        check_vma=False,
    )
```

```python
import functools
import math

import jax
import jax.numpy as jnp
import numpy as np
from jax import lax
from jax.experimental import pallas as pl
from jax.experimental.pallas import tpu as pltpu
from jax.sharding import PartitionSpec as P

HIGHEST = lax.Precision.HIGHEST
HIGHER = lax.Precision.HIGH


def passed_along(x, axis, by):
    length = lax.axis_size(axis)
    return lax.ppermute(x, axis, [(i, (i + by) % length) for i in range(length)])


def make_tables(panel_len):
    span_len = 2 * panel_len
    row_index = lax.broadcasted_iota(jnp.int32, (span_len, panel_len), 0)
    col_index = lax.broadcasted_iota(jnp.int32, (span_len, panel_len), 1)
    frequency = jnp.where(row_index <= panel_len, row_index, row_index - panel_len)
    angles = (frequency * col_index % span_len).astype(jnp.float32) * (2.0 * math.pi / span_len)
    forward_table = jnp.where(row_index <= panel_len, jnp.cos(angles), -jnp.sin(angles))
    end_rows = jnp.logical_or(row_index == 0, row_index == panel_len)
    weights = jnp.where(end_rows, 1.0, 2.0) / span_len
    inverse_table = (forward_table * weights).T
    return (forward_table, inverse_table)


def make_parity(panel_len):
    row_index = lax.broadcasted_iota(jnp.int32, (2 * panel_len, 1), 0)
    frequency = jnp.where(row_index <= panel_len, row_index, row_index - panel_len)
    return (1 - 2 * (frequency % 2)).astype(jnp.float32)


def spec_product(left_spec, right_spec, interior, conjugate):
    panel_len = left_spec.shape[0] // 2
    left_real, left_imag = (left_spec[:panel_len], left_spec[panel_len:])
    right_real, right_imag = (right_spec[:panel_len], right_spec[panel_len:])
    if conjugate:
        right_imag = right_imag * (1.0 - 2.0 * interior)
    real_part = left_real * right_real - interior * left_imag * right_imag
    imag_part = (
        interior * (left_real * right_imag + left_imag * right_real)
        + (1.0 - interior) * left_imag * right_imag
    )
    return jnp.concatenate([real_part, imag_part], axis=0)


def on_device(signal, gate_value, grad_out, long_filter, weight):
    panel_len = signal.shape[1]
    chan_width = signal.shape[2]
    span_len = 2 * panel_len
    panel_count = lax.axis_size("seq")
    my_panel = lax.axis_index("seq")
    forward_table, inverse_table = make_tables(panel_len)
    parity = make_parity(panel_len)
    interior = (lax.broadcasted_iota(jnp.int32, (panel_len, 1), 0) != 0).astype(jnp.float32)
    gated = (gate_value[0].astype(jnp.float32) * grad_out[0].astype(jnp.float32)).astype(
        jnp.bfloat16
    )
    signals, gateds, filters = (
        lax.all_gather(signal, "seq", axis=1, tiled=True),
        lax.all_gather(gated[None], "seq", axis=1, tiled=True),
        lax.all_gather(long_filter, "seq", axis=1, tiled=True),
    )
    zero_spec = jnp.zeros((span_len, chan_width), jnp.float32)

    def spectrum(gathered, panel_at):
        panel_rows = lax.dynamic_slice_in_dim(gathered[0], panel_at * panel_len, panel_len, 0)
        return jnp.dot(forward_table, panel_rows.astype(jnp.float32), precision=HIGHER)

    def spectrum_if(use_panel, gathered, panel_at):
        return lax.cond(
            use_panel,
            lambda where_at: spectrum(gathered, where_at),
            lambda where_at: zero_spec,
            panel_at,
        )

    def invert(spectrum_in):
        return jnp.dot(inverse_table, spectrum_in, precision=HIGHEST)

    def settle(lag_parts, spectrum_in, use_panel, target):

        def add_rows(parts_now):
            row_at = jnp.maximum(target, 0)
            current = lax.dynamic_index_in_dim(parts_now, row_at, 0, keepdims=True)
            return lax.dynamic_update_index_in_dim(
                parts_now, current + invert(spectrum_in)[None], row_at, 0
            )

        return lax.cond(use_panel, add_rows, lambda parts_now: parts_now, lag_parts)

    own_gated = jnp.dot(forward_table, gated.astype(jnp.float32), precision=HIGHER)
    last_lag = jnp.maximum(my_panel, panel_count - 1 - my_panel)
    extras = (
        zero_spec,
        jnp.array(False),
        jnp.zeros((panel_count, panel_len, chan_width), jnp.float32),
    )

    def lag_step(lag_index, loop_state):
        prior_filter, forward_sum, backward_sum, extras_now = loop_state
        filter_now = spectrum(filters, lag_index)
        filter_full = filter_now + parity * prior_filter
        use_forward = lag_index <= my_panel
        use_backward = lag_index <= panel_count - 1 - my_panel
        signal_spec = spectrum_if(use_forward, signals, jnp.maximum(my_panel - lag_index, 0))
        gated_spec = spectrum_if(
            use_backward, gateds, jnp.minimum(my_panel + lag_index, panel_count - 1)
        )
        forward_sum = forward_sum + spec_product(filter_full, signal_spec, interior, False)
        backward_sum = backward_sum + spec_product(gated_spec, filter_full, interior, True)
        prior_pair, prior_flag, lag_parts = extras_now
        pair_spec = spec_product(own_gated, signal_spec, interior, True)
        ready = jnp.logical_and(lag_index >= 1, jnp.logical_or(prior_flag, use_forward))
        lag_parts = settle(lag_parts, prior_pair + parity * pair_spec, ready, lag_index - 1)
        extras_now = (pair_spec, use_forward, lag_parts)
        return (filter_now, forward_sum, backward_sum, extras_now)

    unused_filter, forward_sum, backward_sum, extras = lax.fori_loop(
        0, last_lag + 1, lag_step, (zero_spec, zero_spec, zero_spec, extras)
    )
    prior_pair, prior_flag, lag_parts = extras
    lag_parts = settle(lag_parts, prior_pair, prior_flag, last_lag)
    filter_grad = lax.psum_scatter(
        lag_parts.reshape(1, panel_count * panel_len, chan_width).astype(jnp.bfloat16),
        "seq",
        scatter_dimension=1,
        tiled=True,
    ).astype(jnp.float32)
    conv = invert(forward_sum)
    gate_grad = (grad_out[0].astype(jnp.float32) * conv).astype(jnp.bfloat16)[None]
    signal_grad = invert(backward_sum).astype(jnp.bfloat16)
    received = passed_along(signal_grad[None], "pipe", -1)
    partial_sums = lax.dot_general(
        received[0], weight[0], (((1,), (1,)), ((), ())), preferred_element_type=jnp.float32
    )
    input_grad = lax.psum_scatter(
        partial_sums[None], "chan", scatter_dimension=2, tiled=True
    ).astype(jnp.bfloat16)
    return (gate_grad, filter_grad, input_grad)


MESH = pl.DeviceIdType.MESH
F32 = jnp.float32
BF16 = jnp.bfloat16
CHUNKS = 4
VMEM_BYTES = 62 * 1024 * 1024


def odd_tables(length):
    steps = np.outer(2 * np.arange(length) + 1, np.arange(length)) % (4 * length)
    angles = steps * (math.pi / (2 * length))
    forward = np.concatenate([np.cos(angles), np.sin(angles)], axis=0)
    return forward.astype(BF16), (forward.T / length).astype(BF16)


def dot(a, b):
    return jnp.dot(a, b, preferred_element_type=F32)


def dot_t(a, b):
    return lax.dot_general(a, b, (((1,), (1,)), ((), ())), preferred_element_type=F32)


def relay_order(groups):
    order = []
    for i in range((groups + 1) // 2):
        order += [groups - 1 - i, i]
    return list(dict.fromkeys(order))


def fused_kernel(
    groups, pipes,
    signal, gate_value, grad_out, long_filter, weight, table, inverse,
    gate_grad, filter_grad, input_grad,
    table_v, inverse_v, weight_v, filter_v, signal_v, gated_v, gate_v, grad_v,
    filter_spec, gated_spec, signal_spec, product, sent_v, received_v,
    parts, from_left, from_right, going, gate_grad_v, filter_grad_v, input_grad_v,
    local_sem, seq_send, seq_recv, pipe_send, pipe_recv, going_sem, left_sem, right_sem, out_sem,
):
    rows, width = gate_v.shape
    freqs = table_v.shape[0] // 2
    chunk = rows // CHUNKS
    outs = going.shape[3]
    me_pipe, me_seq, me = lax.axis_index("pipe"), lax.axis_index("seq"), lax.axis_index("chan")
    before = lax.rem(me_pipe + pipes - 1, pipes)
    after = lax.rem(me_pipe + 1, pipes)
    partner = 1 - me_seq
    last = groups - 1

    barrier = pltpu.get_barrier_semaphore()
    greeted = [{"seq": partner}, {"pipe": before}, {"pipe": after}]
    greeted += [{"chan": lax.rem(me + 1, groups)}, {"chan": lax.rem(me + groups - 1, groups)}]
    for device in greeted:
        pl.semaphore_signal(barrier, inc=1, device_id=device, device_id_type=MESH)

    own = pl.ds(pl.multiple_of(me_seq * rows, rows), rows)

    loads = {}
    for i, (name, src, dst) in enumerate([
        ("gate", gate_value.at[0], gate_v),
        ("grad", grad_out.at[0], grad_v),
        ("filter", long_filter.at[0], filter_v.at[own]),
        ("table", table, table_v),
        ("inverse", inverse.at[own], inverse_v),
        ("signal", signal.at[0], signal_v.at[own]),
        ("weight", weight.at[0], weight_v),
    ]):
        loads[name] = pltpu.make_async_copy(src, dst, local_sem.at[i])
        loads[name].start()

    def to_partner(at, src, dst):
        return pltpu.make_async_remote_copy(
            src_ref=src, dst_ref=dst, send_sem=seq_send.at[at], recv_sem=seq_recv.at[at],
            device_id={"seq": partner}, device_id_type=MESH,
        )

    filter_copy = to_partner(0, long_filter.at[0], filter_v.at[own])
    gated_copy = to_partner(1, gated_v.at[own], gated_v.at[own])
    signal_copy = to_partner(2, signal.at[0], signal_v.at[own])
    pl.semaphore_wait(barrier, len(greeted))
    filter_copy.start()
    loads["gate"].wait()
    loads["grad"].wait()
    gated_v[own, :] = (gate_v[...].astype(F32) * grad_v[...].astype(F32)).astype(BF16)
    gated_copy.start()
    signal_copy.start()

    tile = min(256, width)
    tiles = [
        (pl.ds(f, tile), pl.ds(freqs + f, tile), pl.ds(c, tile))
        for c in range(0, width, tile)
        for f in range(0, freqs, tile)
    ]
    loads["table"].wait()
    loads["filter"].wait()
    filter_copy.wait_recv()
    for re, im, ch in tiles:
        filter_spec[re, ch] = dot(table_v[re, :], filter_v[:, ch])
        filter_spec[im, ch] = dot(table_v[im, :], filter_v[:, ch])
    gated_copy.wait_recv()
    for re, im, ch in tiles:
        g_re, g_im = dot(table_v[re, :], gated_v[:, ch]), dot(table_v[im, :], gated_v[:, ch])
        h_re, h_im = filter_spec[re, ch], filter_spec[im, ch]
        gated_spec[re, ch] = g_re
        gated_spec[im, ch] = g_im
        product[re, ch] = (h_re * g_re + h_im * g_im).astype(BF16)
        product[im, ch] = (h_re * g_im - h_im * g_re).astype(BF16)
    loads["inverse"].wait()

    def piece(r):
        return pl.ds(r * chunk, chunk)

    passed = [
        pltpu.make_async_remote_copy(
            src_ref=sent_v.at[piece(r)], dst_ref=received_v.at[piece(r)],
            send_sem=pipe_send.at[r], recv_sem=pipe_recv.at[r],
            device_id={"pipe": before}, device_id_type=MESH,
        )
        for r in range(CHUNKS)
    ]
    half = rows // 2
    for h in range(2):
        at = pl.ds(h * half, half)
        sent_v[at, :] = dot(inverse_v[at, :], product[...]).astype(BF16)
        for r in range(h * CHUNKS // 2, (h + 1) * CHUNKS // 2):
            passed[r].start()

    loads["signal"].wait()
    signal_copy.wait_recv()

    def convolve_start():
        for re, im, ch in tiles:
            s_re, s_im = dot(table_v[re, :], signal_v[:, ch]), dot(table_v[im, :], signal_v[:, ch])
            h_re, h_im = filter_spec[re, ch], filter_spec[im, ch]
            signal_spec[re, ch] = s_re
            signal_spec[im, ch] = s_im
            product[re, ch] = (h_re * s_re - h_im * s_im).astype(BF16)
            product[im, ch] = (h_re * s_im + h_im * s_re).astype(BF16)

    def convolve_end():
        conv = dot(inverse_v[...], product[...])
        gate_grad_v[...] = (grad_v[...].astype(F32) * conv).astype(BF16)
        gate_grad_out.start()

    def correlate():
        for re, im, ch in tiles:
            s_re, s_im = signal_spec[re, ch], signal_spec[im, ch]
            g_re, g_im = gated_spec[re, ch], gated_spec[im, ch]
            product[re, ch] = (s_re * g_re + s_im * g_im).astype(BF16)
            product[im, ch] = (s_re * g_im - s_im * g_re).astype(BF16)
        filter_grad_v[...] = dot(inverse_v[...], product[...])
        filter_grad_out.start()

    gate_grad_out = pltpu.make_async_copy(gate_grad_v, gate_grad.at[0], out_sem.at[0])
    filter_grad_out = pltpu.make_async_copy(filter_grad_v, filter_grad.at[0], out_sem.at[1])
    input_grad_out = [
        pltpu.make_async_copy(
            input_grad_v.at[piece(r)], input_grad.at[0, piece(r)], out_sem.at[2 + r]
        )
        for r in range(CHUNKS)
    ]

    def rightward(r, d):
        return pltpu.make_async_remote_copy(
            src_ref=going.at[r, d], dst_ref=from_left.at[r, d],
            send_sem=going_sem.at[r, d], recv_sem=left_sem.at[r, d],
            device_id={"chan": lax.rem(me + 1, groups)}, device_id_type=MESH,
        )

    def leftward(r, d):
        return pltpu.make_async_remote_copy(
            src_ref=going.at[r, d], dst_ref=from_right.at[r, d],
            send_sem=going_sem.at[r, d], recv_sem=right_sem.at[r, d],
            device_id={"chan": lax.rem(me + groups - 1, groups)}, device_id_type=MESH,
        )

    def multiply(r):
        passed[r].wait_recv()
        block = received_v[piece(r), :]
        for j in range(groups):
            d = jnp.where(2 * me < groups, last - j, j)
            at = pl.ds(pl.multiple_of(d * outs, outs), outs)
            parts[r, d] = dot_t(block, weight_v[at, :])

            @pl.when(jnp.logical_and(me == 0, d > 0))
            def _():
                going[r, d] = parts[r, d].astype(BF16)
                rightward(r, d).start()

            @pl.when(jnp.logical_and(me == last, d < last))
            def _():
                going[r, d] = parts[r, d].astype(BF16)
                leftward(r, d).start()

    def relay(r):
        for d in relay_order(groups):
            @pl.when(jnp.logical_and(me > 0, me < d))
            def _():
                rightward(r, d).wait_recv()
                going[r, d] = (parts[r, d] + from_left[r, d].astype(F32)).astype(BF16)
                rightward(r, d).start()

            @pl.when(jnp.logical_and(me < last, me > d))
            def _():
                leftward(r, d).wait_recv()
                going[r, d] = (parts[r, d] + from_right[r, d].astype(F32)).astype(BF16)
                leftward(r, d).start()

    def finish(r):
        @pl.when(me > 0)
        def _():
            rightward(r, me).wait_recv()
            parts[r, me] = parts[r, me] + from_left[r, me].astype(F32)

        @pl.when(me < last)
        def _():
            leftward(r, me).wait_recv()
            parts[r, me] = parts[r, me] + from_right[r, me].astype(F32)

        input_grad_v[piece(r), :] = parts[r, me].astype(BF16)
        input_grad_out[r].start()

    convolve_start()
    loads["weight"].wait()
    for r in range(CHUNKS):
        multiply(r)
        if r == 1:
            convolve_end()
            correlate()
        if r > 0:
            relay(r - 1)
    finish(0)
    relay(CHUNKS - 1)
    for r in range(1, CHUNKS):
        finish(r)

    for copy in (filter_copy, gated_copy, signal_copy, *passed):
        copy.wait_send()
    for r in range(CHUNKS):
        for d in range(groups):
            @pl.when(me != d)
            def _():
                rightward(r, d).wait_send()
    gate_grad_out.wait()
    filter_grad_out.wait()
    for copy in input_grad_out:
        copy.wait()


def fused(signal, gate_value, grad_out, long_filter, weight):
    groups, pipes = lax.axis_size("chan"), lax.axis_size("pipe")
    _, rows, width = signal.shape
    length = 2 * rows
    model = weight.shape[1]
    outs, chunk = model // groups, rows // CHUNKS
    forward, inverse = odd_tables(length)
    moved = pltpu.VMEM((CHUNKS, groups, chunk, outs), BF16)
    spec = pltpu.VMEM((2 * length, width), F32)
    panel = pltpu.VMEM((rows, width), BF16)
    whole = pltpu.VMEM((length, width), BF16)
    sems = pltpu.SemaphoreType.DMA
    anywhere = pl.BlockSpec(memory_space=pl.ANY)
    macs = 6 * 2 * length * length * width + rows * width * model
    return pl.pallas_call(
        functools.partial(fused_kernel, groups, pipes),
        out_shape=(
            jax.ShapeDtypeStruct((1, rows, width), BF16),
            jax.ShapeDtypeStruct((1, rows, width), F32),
            jax.ShapeDtypeStruct((1, rows, outs), BF16),
        ),
        in_specs=[anywhere] * 7,
        out_specs=(anywhere,) * 3,
        scratch_shapes=[
            pltpu.VMEM((2 * length, length), BF16),
            pltpu.VMEM((rows, 2 * length), BF16),
            pltpu.VMEM((model, width), BF16),
            whole, whole, whole, panel, panel,
            spec, spec, spec,
            pltpu.VMEM((2 * length, width), BF16),
            panel, panel,
            pltpu.VMEM((CHUNKS, groups, chunk, outs), F32),
            moved, moved, moved,
            panel,
            pltpu.VMEM((rows, width), F32),
            pltpu.VMEM((rows, outs), BF16),
            sems((7,)), sems((3,)), sems((3,)), sems((CHUNKS,)), sems((CHUNKS,)),
            sems((CHUNKS, groups)), sems((CHUNKS, groups)), sems((CHUNKS, groups)),
            sems((2 + CHUNKS,)),
        ],
        compiler_params=pltpu.CompilerParams(
            collective_id=0, has_side_effects=True, vmem_limit_bytes=VMEM_BYTES
        ),
        cost_estimate=pl.CostEstimate(flops=2 * macs, bytes_accessed=2 * model * width, transcendentals=0),
    )(signal, gate_value, grad_out, long_filter, weight, jnp.asarray(forward), jnp.asarray(inverse))


def solution(mesh):
    return jax.shard_map(
        fused if mesh.shape["seq"] == 2 else on_device,
        mesh=mesh,
        in_specs=(
            P("pipe", "seq", "chan"),
            P("pipe", "seq", "chan"),
            P("pipe", "seq", "chan"),
            P("pipe", "seq", "chan"),
            P("pipe", None, "chan"),
        ),
        out_specs=(P("pipe", "seq", "chan"), P("pipe", "seq", "chan"), P("pipe", "seq", "chan")),
        check_vma=False,
    )
```
